32 devices in a mesh: layer: 2 (over y), row: 4 (over z), col: 2 (over x), sub: 2 (over core).
Axes of the slice: x: 2, y: 2, z: 4, core: 2. Of those that a mesh axis runs over, the one named last changes fastest.
Arguments:
- act_a: bfloat16 [4, 1024, 14336], P(('layer', 'sub'), 'col', 'row'), parts along dimension 0, may hold values from -4000 to 4000
- act_b: bfloat16 [4, 1024, 14336], P(('layer', 'sub'), 'row', 'col'), parts along dimension 0, may hold values from -4000 to 4000
- pair_index: int32 [28672], P('layer'), parts along dimension 0, may hold values from 0 to 14335, as said below
- weight_a: bfloat16 [28672, 4096], P(('layer', 'row'), ('col', 'sub')), parts along dimension 0, may hold values from -6 to 6
- weight_b: bfloat16 [28672, 4096], P(('layer', 'row'), ('col', 'sub')), parts along dimension 0, may hold values from -6 to 6
Outputs:
- correlation: bfloat16 [28672, 14336], P(('layer', 'row', 'sub'), 'col'), parts along dimension 0
- merged: bfloat16 [28672, 4096], P(('layer', 'row'), ('col', 'sub')), parts along dimension 0
The draws below stay inside these ranges and needn't reach their ends.
There are 2 independent parts, one for each index of `layer`. The reference program is written for one: setup_inputs(seed, part) draws one part's arguments, and reference() takes and returns one part's arrays. A program takes and returns all parts, laid end to end along the dimension named above; each array names one. Nothing has to cross between parts.
Inputs may be any that keep to these rules, and one draw needn't show every extreme that they name: `pair_index`: A permutation of the 14336 units: entry i is the B unit matched to A unit i. Of the 3584 A units of one aligned block, at most 1792 are matched to units of one aligned block of 3584 B units, and in every draw exactly 1792 are for some pair of blocks.
All inputs are finite; a program needn't handle non-finite values.
Results may differ from the reference program's by a relative error of at most 0.007.
Values may be sent and summed in bfloat16 or wider, within the bound.
A program may use at most 320 MiB of HBM per device.

```python
import math
import jax
import jax.numpy as jnp
from jax import lax

U = 14336
DW = 4096
SEQ_LEN = 1024
SEQS = 2
TOKENS = 2048
UNIT_BLOCK = 3584
CAP = 1792


def pair_draw(key):
    key = jax.random.fold_in(key, 101)
    block_count = U // UNIT_BLOCK
    base_count = CAP // 2
    subkeys = jax.random.split(key, 6)
    ordering = jax.random.permutation(subkeys[0], block_count)
    half_base = base_count // 2
    pair_shift = jax.random.randint(subkeys[1], (block_count // 2,), -half_base, half_base + 1)
    pair_shift = pair_shift.at[0].set(base_count)
    pair_load = jnp.zeros((block_count,), jnp.int32)
    pair_load = pair_load.at[ordering[0::2]].set(base_count + pair_shift)
    pair_load = pair_load.at[ordering[1::2]].set(base_count - pair_shift)
    row_label = jax.random.permutation(subkeys[2], block_count)
    col_label = jax.random.permutation(subkeys[3], block_count)
    pair_count = pair_load[jnp.bitwise_xor(row_label[:, None], col_label[None, :])]
    row_end = jnp.cumsum(pair_count, axis=1)
    row_begin = row_end - pair_count
    col_begin = jnp.cumsum(pair_count, axis=0) - pair_count
    slot_index = jnp.arange(UNIT_BLOCK, dtype=jnp.int32)
    source_block = jnp.sum((row_end[:, None, :] <= slot_index[None, :, None]).astype(jnp.int32), axis=2)
    local_b = jnp.take_along_axis(col_begin, source_block, axis=1) + slot_index[None, :] - jnp.take_along_axis(row_begin, source_block, axis=1)
    shuffle_b = jax.vmap(lambda sub_key: jax.random.permutation(sub_key, UNIT_BLOCK))(jax.random.split(subkeys[4], block_count))
    unit_b = source_block * UNIT_BLOCK + shuffle_b[source_block, local_b]
    shuffle_a = jax.vmap(lambda sub_key: jax.random.permutation(sub_key, UNIT_BLOCK))(jax.random.split(subkeys[5], block_count))
    dest_rows = jnp.arange(block_count)[:, None]
    pair_table = jnp.zeros((block_count, UNIT_BLOCK), jnp.int32).at[dest_rows, shuffle_a].set(unit_b)
    return pair_table.reshape(U)


def slab(key, seq_ratio, unit_spread, offset_ratio):
    key = jax.random.fold_in(key, 202)
    subkeys = jax.random.split(key, 9)

    def noise(sub_key):
        gauss = jnp.clip(jax.random.normal(sub_key, (SEQS, SEQ_LEN, U), jnp.float32), -5.0, 5.0)
        return gauss
    seq_pos = jnp.arange(SEQS, dtype=jnp.float32) / max(SEQS - 1, 1)
    seq_scale = jnp.exp(math.log(seq_ratio) * seq_pos)[:, None, None]
    seq_offset = jnp.exp(math.log(offset_ratio) * seq_pos)[:, None, None]
    tok_scale = jnp.exp(jax.random.uniform(subkeys[0], (SEQS, SEQ_LEN, 1), jnp.float32, -0.7, 0.7))
    coupling = jax.random.uniform(subkeys[2], (U,), jnp.float32, -0.4, 0.95)
    first = noise(subkeys[3])
    second = noise(subkeys[4])
    base_a = first
    base_b = coupling * first + jnp.sqrt(1.0 - coupling * coupling) * second
    scale_a = jnp.exp(jax.random.uniform(subkeys[5], (U,), jnp.float32, 0.0, math.log(unit_spread)))
    scale_b = jnp.exp(jax.random.uniform(subkeys[6], (U,), jnp.float32, 0.0, math.log(unit_spread)))
    offset_a = scale_a * jnp.clip(jax.random.normal(subkeys[7], (U,), jnp.float32), -5.0, 5.0)
    offset_b = scale_b * jnp.clip(jax.random.normal(subkeys[8], (U,), jnp.float32), -5.0, 5.0)
    envelope = seq_scale * tok_scale
    values_a = seq_offset * offset_a + scale_a * envelope * base_a
    values_b = seq_offset * offset_b + scale_b * envelope * base_b
    return (values_a, values_b)


def draw_act_a(key, part):
    values_a, values_b = slab(key, 3.0, 10.0, 3.0)
    return values_a.astype(jnp.bfloat16)


def draw_act_b(key, part):
    values_a, values_b = slab(key, 3.0, 10.0, 3.0)
    pairs = pair_draw(key)
    placed = jnp.zeros_like(values_b).at[:, :, pairs].set(values_b)
    return placed.astype(jnp.bfloat16)


def draw_pair_index(key, part):
    return pair_draw(key)


def block_scale(key, dims, shards, least, top_value):
    level = 1.0
    for axis_at, parts in shards:
        steps = jax.random.uniform(jax.random.fold_in(jax.random.fold_in(key, 6), axis_at), (parts,), jnp.float32, least / len(shards), top_value / len(shards))
        level = level * jnp.repeat(jnp.exp(steps), dims[axis_at] // parts).reshape((-1,) + (1,) * (len(dims) - 1 - axis_at))
    return level


def centred(key, dims, spread, most, pieces=(), kind=jnp.bfloat16):
    gain = block_scale(key, dims, pieces, -0.22, 0.18) if pieces else 1.0
    result = jax.random.normal(key, dims, jnp.float32) * spread * gain
    return jnp.minimum(jnp.maximum(result, -most), most).astype(kind)


def setup_inputs(seed: int = 0, part: int = 0) -> dict:
    arg_keys = jax.random.split(jax.random.key(seed), 6)
    part_keys = jax.random.split(jax.random.fold_in(arg_keys[5], part), 6)
    return {
        "act_a": draw_act_a(jax.random.fold_in(jax.random.fold_in(arg_keys[5], part), 71), part),
        "act_b": draw_act_b(jax.random.fold_in(jax.random.fold_in(arg_keys[5], part), 71), part),
        "pair_index": draw_pair_index(jax.random.fold_in(jax.random.fold_in(arg_keys[5], part), 71), part),
        "weight_a": centred(part_keys[3], (U, DW), 1.0, 6.0, ((0, 4), (1, 4))),
        "weight_b": centred(part_keys[4], (U, DW), 1.0, 6.0, ((0, 4), (1, 4))),
    }


EPSILON = 1e-05

def standard(values):
    wide = values.astype(jnp.float32)
    unit_mean = lax.optimization_barrier(jnp.sum(wide, axis=(0, 1))) / TOKENS
    unit_var = lax.optimization_barrier(jnp.sum(jnp.square(wide - unit_mean), axis=(0, 1))) / TOKENS
    return ((wide - unit_mean) * lax.rsqrt(unit_var + EPSILON)).astype(jnp.bfloat16)

def reference(act_a, act_b, pair_index, weight_a, weight_b):
    normed_a = standard(act_a)
    normed_b = standard(act_b)
    row_blocks = normed_a.reshape(SEQS, SEQ_LEN, U // UNIT_BLOCK, UNIT_BLOCK).transpose(2, 0, 1, 3)

    def one_block(portion):
        summed = jnp.zeros((UNIT_BLOCK, U), jnp.float32)
        for sequence in range(SEQS):
            partial_value = jnp.dot(portion[sequence].T, normed_b[sequence], preferred_element_type=jnp.float32) / TOKENS
            rounded = lax.optimization_barrier(partial_value.astype(jnp.bfloat16))
            summed = summed + rounded.astype(jnp.float32)
        return summed.astype(jnp.bfloat16)
    correlation = lax.map(one_block, row_blocks).reshape(U, U)
    matched = correlation[jnp.arange(U), pair_index].astype(jnp.float32)
    share_b = jnp.maximum(matched, 0.0)
    partner = weight_b[pair_index].astype(jnp.float32)
    merged = (weight_a.astype(jnp.float32) + share_b[:, None] * partner) / (1.0 + share_b[:, None])
    return (correlation, merged.astype(jnp.bfloat16))
```

```python
import jax
import jax.numpy as jnp
from jax import lax
from jax.sharding import PartitionSpec as P

EPSILON = 1e-05


def pairs_by_xor(size, step):
    return [(place, place ^ step) for place in range(size)]


def unit_stats(block, axes, count_all):
    wide = block.astype(jnp.float32)
    mean = lax.psum(jnp.sum(wide, axis=0), axes) / count_all
    square = lax.psum(jnp.sum(jnp.square(wide - mean), axis=0), axes)
    return mean, lax.rsqrt(square / count_all + EPSILON)


def normalise(block, stats):
    mean, inverse = stats
    return ((block.astype(jnp.float32) - mean) * inverse).astype(jnp.bfloat16)


def body(act_a, act_b, pair_index, weight_a, weight_b):
    rows, cols, subs = (lax.axis_size(name) for name in ("row", "col", "sub"))
    my_row, my_col, my_sub = (lax.axis_index(name) for name in ("row", "col", "sub"))
    own_a, own_b = act_a[0], act_b[0]
    tokens_a, units_a = own_a.shape
    units_b = own_b.shape[1]
    block = weight_b.shape[0]
    cap = 2 * block // rows
    count_all = float(tokens_a * cols * subs)

    flat_b = lax.all_gather(own_b, "row", axis=0, tiled=True)
    raw_a = jnp.zeros((tokens_a * cols, units_a), own_a.dtype)
    raw_a = lax.dynamic_update_slice_in_dim(raw_a, own_a, my_col * tokens_a, 0)
    for step in range(1, cols):
        came = lax.ppermute(own_a, "col", pairs_by_xor(cols, step))
        raw_a = lax.dynamic_update_slice_in_dim(raw_a, came, (my_col ^ step) * tokens_a, 0)

    def rank_in(mask):
        return jnp.cumsum(mask.astype(jnp.int32)) - 1

    def packed(step):
        theirs = lax.dynamic_slice_in_dim(pair_index, (my_row ^ step) * block, block)
        local = theirs - my_row * block
        mask = (local >= 0) & (local < block)
        place = jnp.where(mask, rank_in(mask), -1)
        hit = place[None, :] == jnp.arange(cap, dtype=jnp.int32)[:, None]
        chosen = jnp.sum(jnp.where(hit, local[None, :], 0), axis=1)
        return weight_b.at[chosen].get(mode="promise_in_bounds")

    early = [rows // 2]
    late = [step for step in range(rows - 1, 0, -1) if step not in early]
    arrived = {}
    for step in early:
        arrived[step] = lax.ppermute(packed(step), "row", pairs_by_xor(rows, step))
    waiting = [packed(step) for step in late]

    stats_a = unit_stats(own_a, ("col", "sub"), count_all)
    stats_b = unit_stats(own_b, ("row", "sub"), count_all)

    flat_b, *waiting = lax.optimization_barrier((flat_b, *waiting))
    for step, rows_out in zip(late, waiting):
        arrived[step] = lax.ppermute(rows_out, "row", pairs_by_xor(rows, step))

    normed_a = normalise(raw_a, stats_a)
    normed_b = normalise(flat_b, stats_b)
    kept_rows = units_a // subs
    product = lax.dot_general(
        normed_a, normed_b, (((0,), (0,)), ((), ())), preferred_element_type=jnp.float32
    )
    correlation = lax.psum_scatter(
        (product / count_all).astype(jnp.bfloat16), "sub", scatter_dimension=0, tiled=True
    )
    row_start = my_row * units_a + my_sub * kept_rows
    my_pairs = lax.dynamic_slice_in_dim(pair_index, row_start, kept_rows)
    local_col = my_pairs - my_col * units_b
    inside = (local_col >= 0) & (local_col < units_b)
    picked_values = jnp.take_along_axis(
        correlation, jnp.clip(local_col, 0, units_b - 1)[:, None], axis=1
    )[:, 0]
    own_terms = jnp.where(inside, picked_values.astype(jnp.float32), 0.0)
    spread = lax.dynamic_update_slice_in_dim(
        jnp.zeros((units_a,), jnp.float32), own_terms, my_sub * kept_rows, 0
    )
    matched = lax.psum(spread, ("col", "sub"))
    share_b = jnp.maximum(matched, 0.0)

    unit_pairs = lax.dynamic_slice_in_dim(pair_index, my_row * units_a, units_a)
    local = unit_pairs - my_row * block
    mask = (local >= 0) & (local < block)
    spot = jnp.where(mask, local, 0)
    table = [weight_b]
    start = block
    for step in early + late:
        table.append(arrived[step])
        theirs = unit_pairs - (my_row ^ step) * block
        mask = (theirs >= 0) & (theirs < block)
        spot = jnp.where(mask, start + rank_in(mask), spot)
        start += cap
    portion = jnp.concatenate(table, axis=0)
    partner = portion.at[spot].get(mode="promise_in_bounds").astype(jnp.float32)
    merged = (weight_a.astype(jnp.float32) + share_b[:, None] * partner) / (1.0 + share_b[:, None])
    return (correlation, merged.astype(jnp.bfloat16))


def solution(mesh):
    return jax.shard_map(
        body,
        mesh=mesh,
        in_specs=(
            P(("layer", "sub"), "col", "row"),
            P(("layer", "sub"), "row", "col"),
            P("layer"),
            P(("layer", "row"), ("col", "sub")),
            P(("layer", "row"), ("col", "sub")),
        ),
        out_specs=(P(("layer", "row", "sub"), "col"), P(("layer", "row"), ("col", "sub"))),
        check_vma=False,
    )
```
